32 devices in a mesh: groups: 2 (over y), side: 2 (over core), member: 8 (over z, x).
Axes of the slice: x: 2, y: 2, z: 4, core: 2. Of those that a mesh axis runs over, the one named last changes fastest.
Arguments:
- queries: bfloat16 [192, 64, 576], P(('groups', 'side', 'member')), parts along dimension 0, may hold values from -16 to 16
- latent_cache: bfloat16 [192, 128, 576], P(('groups', 'side', 'member')), parts along dimension 0, may hold values from -6 to 6
- lengths: int32 [192], P(('groups', 'side', 'member')), parts along dimension 0, may hold values from 1 to 128, 7680 in all
- moe_input: bfloat16 [192, 3584], P(('groups', 'side', 'member')), parts along dimension 0, may hold values from -6 to 6
- expert_ids: int32 [192, 8], P(('groups', 'side', 'member')), parts along dimension 0, may hold values from 0 to 31, all different within a row; in each aligned block of 6 rows (0 to 5, 6 to 11, ...) at most 2 rows name the same one
- route_scores: float32 [192, 8], P(('groups', 'side', 'member')), parts along dimension 0, may hold values from 0.05 to 1
- placement: int32 [32], replicated, may hold values from 0 to 31, each once
- w_gate: bfloat16 [32, 3584, 2048], P(('side', 'member')), may hold values from -0.09375 to 0.09375
- w_up: bfloat16 [32, 3584, 2048], P(('side', 'member')), may hold values from -0.09375 to 0.09375
- w_down: bfloat16 [32, 2048, 3584], P(('side', 'member')), may hold values from -0.125 to 0.125
Outputs:
- latent_out: bfloat16 [192, 64, 512], P(('groups', 'side', 'member')), parts along dimension 0
- moe_out: bfloat16 [192, 3584], P(('groups', 'side', 'member')), parts along dimension 0
The draws below stay inside these ranges and needn't reach their ends.
There are 2 independent parts, one for each index of `groups`. The reference program is written for one: setup_inputs(seed, part) draws one part's arguments, and reference() takes and returns one part's arrays. A program takes and returns all parts, laid end to end along the dimension named above; an argument that names none is the same for every part. Nothing has to cross between parts.
Inputs may be any that keep to these rules, and one draw needn't show every extreme that they name: `expert_ids`: each row names 8 different experts. Within the rows of one device (aligned blocks of 6 rows) no expert is named by more than 2 rows, a bound that some block reaches. Some request has length exactly 128. The lengths of one part sum to 7680; each part is drawn on its own. `placement`: each slot holds one expert.
All inputs are finite; a program needn't handle non-finite values. No bound on the sum of `lengths` on one device may be relied on, other than what follows from the above.
Results may differ from the reference program's by a relative error of at most 0.0085.
Values may be sent and summed in bfloat16 or wider, within the bound.
A program may use at most 192 MiB of HBM per device.

```python
import math
import jax
import jax.numpy as jnp
import numpy as np
from jax import lax

D = 3584
FF = 2048
HEADS = 64
LATENT = 512
ROPE = 64
QK_DIM = 192
EXPERTS = 32
ROUTED = 8
REQ_DEV = 6
CTX = 128
REQUESTS = 96
CAP = 2
SPLIT = 1
PIECES = 32
N_SIDE = 2
N_MEMBER = 8


def cache_parts(key):
    entry_width = LATENT + ROPE
    normal_base = jnp.clip(jax.random.normal(jax.random.fold_in(key, 101), (REQUESTS, CTX, entry_width), jnp.float32), -6.0, 6.0)
    return normal_base


def draw_latent_cache(key, part):
    normal_base = cache_parts(key)
    return normal_base.astype(jnp.bfloat16)


def draw_queries(key, part):
    key = jax.random.fold_in(key, 9)
    entry_width = LATENT + ROPE
    return jnp.clip(jax.random.normal(key, (REQUESTS, HEADS, entry_width), jnp.float32), -6.0, 6.0).astype(jnp.bfloat16)


def shard_levels(rng, shape, split, least, top_value):
    gain, own = 1.0, jax.random.fold_in(rng, 6)
    for axis_at, blocks in split:
        draws = jnp.exp(jax.random.uniform(jax.random.fold_in(own, axis_at), (blocks,), jnp.float32, least / len(split), top_value / len(split)))
        gain = gain * jnp.repeat(draws, shape[axis_at] // blocks).reshape([-1 if axis == axis_at else 1 for axis in range(len(shape))])
    return gain


def profile(amount, total, limit, skew):
    weights = [(1 << 20) // math.isqrt(standing ** skew) + 1 for standing in range(2, amount + 1)]
    rest, given = total - limit - (amount - 1), [1] * (amount - 1)
    while rest > 0:
        movable = [i for i in range(amount - 1) if given[i] < limit]
        mass, remaining = sum([weights[i] for i in movable]), rest
        for i in movable:
            more = min(limit - given[i], max(1, remaining * weights[i] // mass), rest)
            given[i] = given[i] + more
            rest = rest - more
    return np.array([limit] + given)


def ragged(own_key, count, total, limit, slope):
    if count == 2:
        one = jax.random.randint(own_key, (), max(1, total - limit), min(limit, total - 1) + 1)
        return jnp.stack([one, total - one])
    tallies = jnp.asarray(profile(count, total, limit, slope), jnp.int32)
    couples = (count - 1) // 2
    source_of, sink = tallies[1:1 + 2 * couples:2], tallies[2:2 + 2 * couples:2]
    slack = jnp.minimum(source_of - 1, limit - sink)
    moved = jax.random.randint(jax.random.fold_in(own_key, 1), (couples,), 0, 1 << 20) % (slack + 1)
    tallies = tallies.at[1:1 + 2 * couples:2].set(source_of - moved).at[2:2 + 2 * couples:2].set(sink + moved)
    return tallies[jax.random.permutation(jax.random.fold_in(own_key, 2), count)]


def deal_out(stream_key, own, number, rows, count, top, most, lean):
    order = jax.random.permutation(stream_key, count)
    heavy_load, ordinary = load_shares(count, rows * top, most, lean, True), load_shares(count, rows * top, most, lean, False)
    places = jnp.arange(count)

    def named(sizes, offset_by):
        used = int((sizes > 0).sum())
        fixed = max(1, used // 4)
        moved = fixed + (places - fixed + offset_by * (used - fixed)) % max(1, count - fixed)
        return jnp.zeros((count,), jnp.int32).at[order[jnp.where(places < fixed, places, moved)]].set(jnp.asarray(sizes, jnp.int32))

    sizes = jnp.where(number % 4 == 0, named(heavy_load, number // 4), named(ordinary, number - number // 4 - 1))
    mixed = jax.random.permutation(jax.random.fold_in(own, 3), count)
    source_of, taker = mixed[0:count // 2 * 2:2], mixed[1:count // 2 * 2:2]
    slack = jnp.minimum(sizes[source_of] - 1, most - sizes[taker]) // 2
    slack = jnp.where((source_of == order[0]) | (taker == order[0]) | (sizes[taker] == 0), 0, jnp.maximum(slack, 0))
    moved = jax.random.randint(jax.random.fold_in(own, 4), (count // 2,), 0, 1 << 20) % (slack + 1)
    sizes = sizes.at[source_of].add(-moved).at[taker].add(moved)
    members = jnp.searchsorted(jnp.cumsum(sizes), jnp.arange(rows * top), side="right").astype(jnp.int32)
    table = members.reshape(top, rows).T
    table = table[jax.random.permutation(jax.random.fold_in(own, 1), rows)]
    offset_by = jax.random.randint(jax.random.fold_in(own, 2), (rows, 1), 0, top)
    return jnp.take_along_axis(table, (jnp.arange(top)[None, :] + offset_by) % top, axis=1)


def load_shares(number_of, total, limit, slope, full):
    weights = [(1 << 20) // math.isqrt(grade ** slope) + 1 for grade in range(1, number_of + 1)]
    largest = limit if full else min(limit, max(-(-total // number_of), total * weights[0] // sum(weights)))
    least = 1 if total - largest >= number_of - 1 else 0
    holding, rest = [largest] + [least] * (number_of - 1), total - largest - least * (number_of - 1)
    while rest > 0:
        candidates = [i for i in range(1, number_of) if holding[i] < largest] or [i for i in range(1, number_of) if holding[i] < limit]
        whole, left = sum([weights[i] for i in candidates]), rest
        for i in candidates:
            addition = min(limit - holding[i], max(1, left * weights[i] // whole), rest)
            holding[i] = holding[i] + addition
            rest = rest - addition
    return np.array(holding)


def centred(key, extent, scale, limit, pieces=(), kind=jnp.bfloat16):
    entries = scale * jax.random.normal(key, extent, jnp.float32)
    if pieces:
        entries = entries * shard_levels(key, extent, pieces, -0.22, 0.18)
    return jnp.clip(entries, -limit, limit).astype(kind)


def setup_inputs(seed: int = 0, part: int = 0) -> dict:
    splits = jax.random.split(jax.random.key(seed), 11)
    part_keys = jax.random.split(jax.random.fold_in(splits[10], part), 11)
    queries = draw_queries(jax.random.fold_in(jax.random.fold_in(splits[10], part), 71), part)
    latent_cache = draw_latent_cache(jax.random.fold_in(jax.random.fold_in(splits[10], part), 71), part)
    lengths = ragged(part_keys[2], REQUESTS, REQUESTS * CTX * 5 // 8, CTX, 2).astype(jnp.int32)
    moe_input = centred(part_keys[3], (REQUESTS, D), 1.0, 6.0, ((0, 16),))
    expert_ids_keys = jax.random.split(jax.random.fold_in(part_keys[4], 1), REQUESTS // REQ_DEV)
    expert_ids_turns = jax.random.permutation(jax.random.fold_in(part_keys[4], 3), REQUESTS // REQ_DEV)
    expert_ids = jax.vmap(lambda own, number: deal_out(jax.random.fold_in(part_keys[4], 2), own, number, REQ_DEV, EXPERTS, ROUTED, CAP, 2))(expert_ids_keys, expert_ids_turns).reshape((REQUESTS, ROUTED))
    route_scores = jnp.clip(jnp.exp(math.log(1.0) - 2.9957323 * jax.random.uniform(part_keys[5], (REQUESTS, ROUTED), jnp.float32) ** shard_levels(part_keys[5], (REQUESTS, ROUTED), ((0, 16),), -0.2, 0.2)), 0.05, 1.0)
    placement = jax.random.permutation(splits[6], EXPERTS).astype(jnp.int32)
    w_gate = centred(splits[7], (PIECES, D, FF // SPLIT), D ** -0.5, 0.09375, ((0, 16),))
    w_up = centred(splits[8], (PIECES, D, FF // SPLIT), D ** -0.5, 0.09375, ((0, 16),))
    w_down = centred(splits[9], (PIECES, FF // SPLIT, D), FF ** -0.5, 0.125, ((0, 16),))
    return dict(queries=queries, latent_cache=latent_cache, lengths=lengths, moe_input=moe_input, expert_ids=expert_ids, route_scores=route_scores, placement=placement, w_gate=w_gate, w_up=w_up, w_down=w_down)


def attend(queries, latent_cache, lengths):
    score_scale = QK_DIM ** -0.5
    scores = jnp.einsum('rhc,rtc->rht', queries.astype(jnp.float32), latent_cache.astype(jnp.float32), precision=lax.Precision.HIGHEST) * score_scale
    is_valid = jnp.arange(CTX, dtype=jnp.int32)[None, None, :] < lengths.astype(jnp.int32)[:, None, None]
    scores = jnp.where(is_valid, scores, -jnp.inf)
    row_max = jnp.max(scores, axis=2, keepdims=True)
    exp_scores = jnp.exp(scores - row_max)
    row_total = jnp.sum(exp_scores, axis=2, keepdims=True)
    attn_weights = (exp_scores / row_total).astype(jnp.bfloat16)
    values = latent_cache[:, :, :LATENT].astype(jnp.float32)
    latent_out = jnp.einsum('rht,rtc->rhc', attn_weights.astype(jnp.float32), values, precision=lax.Precision.HIGHEST)
    return latent_out.astype(jnp.bfloat16)


def routing(expert_ids, route_scores, placement):
    experts = placement.shape[0]
    slot_table = (placement[:, None] == jnp.arange(experts, dtype=jnp.int32)[None, :]).astype(jnp.float32)
    picked = (expert_ids[:, :, None] == jnp.arange(experts, dtype=jnp.int32)[None, None, :]).astype(jnp.float32)
    chosen = jnp.einsum('tke,es->tks', picked, slot_table, precision=lax.Precision.HIGHEST)
    scaled = 2.5 * route_scores / jnp.sum(route_scores, axis=1, keepdims=True)
    taken_slots = jnp.sum(chosen, axis=1)
    slot_weight = jnp.einsum('tk,tks->ts', scaled, chosen, precision=lax.Precision.HIGHEST)
    return taken_slots, slot_weight


def reference(queries, latent_cache, lengths, moe_input, expert_ids, route_scores, placement, w_gate, w_up, w_down):
    latent_out = attend(queries, latent_cache, lengths)
    taken_slots, slot_weight = routing(expert_ids, route_scores, placement)
    tokens, model_width = moe_input.shape
    row_bound = N_SIDE * N_MEMBER * CAP
    piece_width = FF // SPLIT

    def one_slot(slot_index, running):
        slot_index = jnp.asarray(slot_index).astype(jnp.int32)
        routed_mask = taken_slots[:, slot_index] > 0.5
        row_index = jnp.nonzero(routed_mask, size=row_bound, fill_value=0)[0].astype(jnp.int32)
        is_live = jnp.arange(row_bound, dtype=jnp.int32) < jnp.sum(routed_mask.astype(jnp.int32))
        token_rows = moe_input[row_index]
        first_piece = (slot_index * SPLIT).astype(jnp.int32)
        gate_full = jnp.transpose(lax.dynamic_slice_in_dim(w_gate, first_piece, SPLIT, 0), (1, 0, 2)).reshape(model_width, FF)
        up_full = jnp.transpose(lax.dynamic_slice_in_dim(w_up, first_piece, SPLIT, 0), (1, 0, 2)).reshape(model_width, FF)
        down_pieces = lax.dynamic_slice_in_dim(w_down, first_piece, SPLIT, 0)
        gate_acts = jnp.dot(token_rows, gate_full, preferred_element_type=jnp.float32)
        up_acts = jnp.dot(token_rows, up_full, preferred_element_type=jnp.float32)
        inner = (jax.nn.silu(gate_acts) * up_acts).astype(jnp.bfloat16)
        inner_pieces = inner.reshape(row_bound, SPLIT, piece_width)
        piece_out = jnp.einsum('rsf,sfd->rsd', inner_pieces.astype(jnp.float32), down_pieces.astype(jnp.float32), precision=lax.Precision.HIGHEST)
        piece_out = lax.optimization_barrier(piece_out.astype(jnp.bfloat16))
        expert_out = jnp.sum(piece_out.astype(jnp.float32), axis=1)
        factor = jnp.where(is_live, slot_weight[row_index, slot_index], jnp.zeros((), jnp.float32))
        return running.at[row_index].add(expert_out * factor[:, None])

    moe_sum = lax.fori_loop(0, EXPERTS, one_slot, jnp.zeros((tokens, model_width), jnp.float32))
    return latent_out, moe_sum.astype(jnp.bfloat16)
```

```python
import functools

import jax
import jax.numpy as jnp
from jax import lax
from jax.experimental import pallas as pl
from jax.experimental.pallas import tpu as pltpu
from jax.sharding import PartitionSpec as P

LATENT = 512
QK_DIM = 192
CHUNK = 512
MESH = pl.DeviceIdType.MESH


def row_tables(placement_ref, ids, scores, n, pieces, cap, experts, rows):
    split = n * pieces // experts
    tokens, routed = ids.shape
    lanes = lax.broadcasted_iota(jnp.int32, (8, rows), 1).astype(jnp.float32)
    block = jnp.floor((lanes + 0.5) * (1.0 / cap))
    position = lanes - cap * block
    piece = jnp.floor((block + 0.5) * (1.0 / n))
    device = block - n * piece
    slot = jnp.floor((device * pieces + piece + 0.5) * (1.0 / split)).astype(jnp.int32)
    expert = jnp.full((8, rows), -1, jnp.int32)
    for e in range(experts):
        expert = jnp.where(slot == placement_ref[e], e, expert)
    expert, position = expert[:tokens], position[:tokens]
    mix = 2.5 * scores / jnp.sum(scores, axis=1, keepdims=True)
    hits = jnp.zeros((tokens, rows), jnp.float32)
    weight = jnp.zeros((tokens, rows), jnp.float32)
    for k in range(routed):
        same = ids[:, k : k + 1] == expert
        hits = jnp.where(same, 1.0, hits)
        weight = jnp.where(same, mix[:, k : k + 1], weight)
    token = lax.broadcasted_iota(jnp.int32, (tokens, rows), 0)
    earlier = jnp.zeros((tokens, rows), jnp.float32)
    for t in range(tokens - 1):
        earlier = earlier + jnp.where(token > t, hits[t : t + 1], 0.0)
    place = jnp.where(earlier == position, hits, 0.0)
    return place, place * weight


def kernel(
    n, n_member, pieces, cap, experts,
    placement_ref, lengths_ref, ids_ref, scores_ref, x_ref,
    q_hbm, c_hbm, wg_hbm, wu_hbm, wd_hbm,
    latent_hbm, moe_ref,
    q_ref, c_ref, o_ref, wg_ref, wu_ref, wd_ref,
    xs_ref, send_ref, arr_ref, x2_ref, ag_ref, au_ref, inner_ref, yb_ref, ret_ref, mixw_ref, out_ref,
    q_sem, c_sem, o_sem, wg_sem, wu_sem, wd_sem,
    dsend_sem, drecv_sem, rsend_sem, rrecv_sem,
):
    side, member = lax.axis_index("side"), lax.axis_index("member")
    me = side * n_member + member
    tokens, width = x_ref.shape
    hidden = wg_hbm.shape[2]
    requests = q_hbm.shape[0]
    rows = pieces * n * cap
    per = n * cap
    nk = width // CHUNK

    def peer(i):
        d = lax.rem(me + i, n)
        return d, {"side": d // n_member, "member": lax.rem(d, n_member)}

    def gate_copy(p, i):
        return pltpu.make_async_copy(
            wg_hbm.at[p, pl.ds(pl.multiple_of(i * CHUNK, CHUNK), CHUNK)], wg_ref.at[i], wg_sem.at[i]
        )

    def up_copy(p, i):
        return pltpu.make_async_copy(
            wu_hbm.at[p, pl.ds(pl.multiple_of(i * CHUNK, CHUNK), CHUNK)], wu_ref.at[i], wu_sem.at[i]
        )

    def down_copy(p, i):
        return pltpu.make_async_copy(
            wd_hbm.at[p, :, pl.ds(pl.multiple_of(i * CHUNK, CHUNK), CHUNK)], wd_ref.at[i], wd_sem.at[i]
        )

    barrier = pltpu.get_barrier_semaphore()

    @pl.loop(1, n)
    def _(i):
        pl.semaphore_signal(barrier, inc=1, device_id=peer(i)[1], device_id_type=MESH)

    q_copy = pltpu.make_async_copy(q_hbm, q_ref, q_sem)
    c_copy = pltpu.make_async_copy(c_hbm, c_ref, c_sem)
    o_copy = pltpu.make_async_copy(o_ref, latent_hbm, o_sem)
    q_copy.start()
    c_copy.start()

    @pl.loop(0, nk)
    def _(i):
        gate_copy(0, i).start()
        up_copy(0, i).start()

    @pl.loop(0, nk)
    def _(i):
        down_copy(0, i).start()

    lanes = -(-rows // 128) * 128
    place, mixw = row_tables(
        placement_ref, ids_ref[...], scores_ref[...], n, pieces, cap, experts, lanes
    )
    high = mixw.astype(jnp.bfloat16)
    rest = mixw - high.astype(jnp.float32)
    mid = rest.astype(jnp.bfloat16)
    low = (rest - mid.astype(jnp.float32)).astype(jnp.bfloat16)
    pad = jnp.zeros((8 - tokens, lanes), jnp.float32)
    mixw_ref[...] = jnp.concatenate(
        [
            jnp.concatenate([v.astype(jnp.float32), pad], axis=0)
            for v in (high, mid, low, jnp.zeros_like(low))
        ],
        axis=0,
    ).astype(jnp.bfloat16)
    picks = jnp.concatenate([place, jnp.zeros((16 - tokens, lanes), jnp.float32)], axis=0)
    picks = picks.T.astype(jnp.bfloat16)
    xs_ref[...] = jnp.zeros_like(xs_ref)
    xs_ref[0:tokens, :] = x_ref[...]
    for p in range(pieces):
        for j in range(nk):
            cols = pl.ds(j * CHUNK, CHUNK)
            made = jnp.dot(
                picks[p * per : (p + 1) * per], xs_ref[:, cols], preferred_element_type=jnp.float32
            )
            send_ref[p, :, :, cols] = made.reshape(n, cap, CHUNK).astype(jnp.bfloat16)

    pl.semaphore_wait(barrier, n - 1)
    for p in range(pieces):

        @pl.loop(1, n)
        def _(i, p=p):
            d, where = peer(i)
            pltpu.make_async_remote_copy(
                src_ref=send_ref.at[p, d],
                dst_ref=arr_ref.at[p, me],
                send_sem=dsend_sem.at[p],
                recv_sem=drecv_sem.at[p],
                device_id=where,
                device_id_type=MESH,
            ).start()

        arr_ref[p, me] = send_ref[p, me]

    q_copy.wait()
    c_copy.wait()
    scale = QK_DIM ** (-0.5)
    for r in range(requests):
        s = lax.dot_general(
            q_ref[r], c_ref[r], (((1,), (1,)), ((), ())), preferred_element_type=jnp.float32
        ) * scale
        valid = lax.broadcasted_iota(jnp.int32, s.shape, 1) < lengths_ref[r]
        s = jnp.where(valid, s, -jnp.inf)
        e = jnp.exp(s - jnp.max(s, axis=1, keepdims=True))
        a = (e / jnp.sum(e, axis=1, keepdims=True)).astype(jnp.bfloat16)
        o_ref[r] = jnp.dot(
            a, c_ref[r, :, :LATENT], preferred_element_type=jnp.float32
        ).astype(jnp.bfloat16)
    o_copy.start()

    def all_but_one(ref):
        return ref.at[pl.ds(0, n - 1)]

    def drain(ref, sem):
        view = all_but_one(ref)
        pltpu.make_async_copy(view, view, sem).wait()

    def combine(p, j):
        drain(ret_ref.at[p, j], rrecv_sem.at[p, j])
        got = ret_ref[p, j].astype(jnp.float32).reshape(per, CHUNK).astype(jnp.bfloat16)
        part = jnp.dot(
            mixw_ref[:, p * per : (p + 1) * per], got, preferred_element_type=jnp.float32
        )
        part = part[0:8] + part[8:16] + part[16:24]
        return part

    for p in range(pieces):
        drain(arr_ref.at[p], drecv_sem.at[p])
        for j in range(nk):
            cols = pl.ds(j * CHUNK, CHUNK)
            x2_ref[:, cols] = (
                arr_ref[p, :, :, cols].astype(jnp.float32).reshape(per, CHUNK).astype(jnp.bfloat16)
            )
        ag_ref[...] = jnp.zeros_like(ag_ref)
        au_ref[...] = jnp.zeros_like(au_ref)

        @pl.loop(0, nk)
        def _(i, p=p):
            xk = x2_ref[:, pl.ds(pl.multiple_of(i * CHUNK, CHUNK), CHUNK)]
            gate_copy(p, i).wait()
            ag_ref[...] += jnp.dot(xk, wg_ref[i], preferred_element_type=jnp.float32)
            if p + 1 < pieces:
                gate_copy(p + 1, i).start()
            up_copy(p, i).wait()
            au_ref[...] += jnp.dot(xk, wu_ref[i], preferred_element_type=jnp.float32)
            if p + 1 < pieces:
                up_copy(p + 1, i).start()

        g = ag_ref[...]
        inner_ref[...] = (g / (1.0 + jnp.exp(-g)) * au_ref[...]).astype(jnp.bfloat16)
        if p > 0:
            for j in range(nk):
                cols = pl.ds(j * CHUNK, CHUNK)
                before = 0.0 if p == 1 else out_ref[:, cols]
                out_ref[:, cols] = before + combine(p - 1, j)

        @pl.loop(0, nk)
        def _(j, p=p):
            down_copy(p, j).wait()
            y = jnp.dot(inner_ref[...], wd_ref[j], preferred_element_type=jnp.float32)
            if p + 1 < pieces:
                down_copy(p + 1, j).start()
            yb_ref[p, j] = y.reshape(n, cap, CHUNK).astype(jnp.bfloat16)

            @pl.loop(1, n)
            def _(i):
                d, where = peer(i)
                pltpu.make_async_remote_copy(
                    src_ref=yb_ref.at[p, j, d],
                    dst_ref=ret_ref.at[p, j, me],
                    send_sem=rsend_sem.at[p, j],
                    recv_sem=rrecv_sem.at[p, j],
                    device_id=where,
                    device_id_type=MESH,
                ).start()

            ret_ref[p, j, me] = yb_ref[p, j, me]

    last = pieces - 1
    for j in range(nk):
        cols = pl.ds(j * CHUNK, CHUNK)
        total = combine(last, j)
        if pieces > 1:
            total = total + out_ref[:, cols]
        moe_ref[:, cols] = total[0:tokens].astype(jnp.bfloat16)

    o_copy.wait()
    for p in range(pieces):
        drain(send_ref.at[p], dsend_sem.at[p])

        @pl.loop(0, nk)
        def _(j, p=p):
            drain(yb_ref.at[p, j], rsend_sem.at[p, j])


def shards(
    queries,
    latent_cache,
    lengths,
    moe_input,
    expert_ids,
    route_scores,
    placement,
    w_gate,
    w_up,
    w_down,
):
    n_side, n_member = lax.axis_size("side"), lax.axis_size("member")
    n = n_side * n_member
    pieces, width, hidden = w_gate.shape
    experts = placement.shape[0]
    tokens = moe_input.shape[0]
    cap = tokens * expert_ids.shape[1] // experts + 1
    per = n * cap
    rows = pieces * per
    lanes = -(-rows // 128) * 128
    nk = width // CHUNK
    requests, heads, entry = queries.shape
    bf16, f32 = jnp.bfloat16, jnp.float32
    vmem = pl.BlockSpec(memory_space=pltpu.VMEM)
    smem = pl.BlockSpec(memory_space=pltpu.SMEM)
    hbm = pl.BlockSpec(memory_space=pl.ANY)
    dma = pltpu.SemaphoreType.DMA
    latent_out, moe_out = pl.pallas_call(
        functools.partial(kernel, n, n_member, pieces, cap, experts),
        out_shape=(
            jax.ShapeDtypeStruct((requests, heads, LATENT), bf16),
            jax.ShapeDtypeStruct((tokens, width), bf16),
        ),
        in_specs=[smem, smem, vmem, vmem, vmem, hbm, hbm, hbm, hbm, hbm],
        out_specs=(hbm, vmem),
        scratch_shapes=[
            pltpu.VMEM(queries.shape, bf16),
            pltpu.VMEM(latent_cache.shape, bf16),
            pltpu.VMEM((requests, heads, LATENT), bf16),
            pltpu.VMEM((nk, CHUNK, hidden), bf16),
            pltpu.VMEM((nk, CHUNK, hidden), bf16),
            pltpu.VMEM((nk, hidden, CHUNK), bf16),
            pltpu.VMEM((16, width), bf16),
            pltpu.VMEM((pieces, n, cap, width), bf16),
            pltpu.VMEM((pieces, n, cap, width), bf16),
            pltpu.VMEM((per, width), bf16),
            pltpu.VMEM((per, hidden), f32),
            pltpu.VMEM((per, hidden), f32),
            pltpu.VMEM((per, hidden), bf16),
            pltpu.VMEM((pieces, nk, n, cap, CHUNK), bf16),
            pltpu.VMEM((pieces, nk, n, cap, CHUNK), bf16),
            pltpu.VMEM((32, lanes), bf16),
            pltpu.VMEM((8, width), f32),
            dma,
            dma,
            dma,
            dma((nk,)),
            dma((nk,)),
            dma((nk,)),
            dma((pieces,)),
            dma((pieces,)),
            dma((pieces, nk)),
            dma((pieces, nk)),
        ],
        compiler_params=pltpu.CompilerParams(
            collective_id=0, has_side_effects=True, vmem_limit_bytes=60 * 1024 * 1024
        ),
        cost_estimate=pl.CostEstimate(
            flops=6 * rows * width * hidden,
            bytes_accessed=6 * pieces * width * hidden,
            transcendentals=per * hidden,
        ),
    )(
        placement,
        lengths,
        expert_ids,
        route_scores,
        moe_input,
        queries,
        latent_cache,
        w_gate,
        w_up,
        w_down,
    )
    return (latent_out, moe_out)


def solution(mesh):
    return jax.shard_map(
        shards,
        mesh=mesh,
        in_specs=(
            P(("groups", "side", "member"), None, None),
            P(("groups", "side", "member"), None, None),
            P(("groups", "side", "member")),
            P(("groups", "side", "member"), None),
            P(("groups", "side", "member"), None),
            P(("groups", "side", "member"), None),
            P(),
            P(("side", "member"), None, None),
            P(("side", "member"), None, None),
            P(("side", "member"), None, None),
        ),
        out_specs=(
            P(("groups", "side", "member"), None, None),
            P(("groups", "side", "member"), None),
        ),
        check_vma=False,
    )
```

```python
import functools

import jax
import jax.numpy as jnp
from jax import lax
from jax.experimental import pallas as pl
from jax.experimental.pallas import tpu as pltpu
from jax.sharding import PartitionSpec as P

LATENT = 512
QK_DIM = 192
CHUNK = 512
MESH = pl.DeviceIdType.MESH


def row_tables(placement_ref, ids, scores, n, pieces, cap, experts, rows):
    split = n * pieces // experts
    tokens, routed = ids.shape
    lanes = lax.broadcasted_iota(jnp.int32, (8, rows), 1).astype(jnp.float32)
    block = jnp.floor((lanes + 0.5) * (1.0 / cap))
    position = lanes - cap * block
    piece = jnp.floor((block + 0.5) * (1.0 / n))
    device = block - n * piece
    slot = jnp.floor((device * pieces + piece + 0.5) * (1.0 / split)).astype(jnp.int32)
    expert = jnp.full((8, rows), -1, jnp.int32)
    for e in range(experts):
        expert = jnp.where(slot == placement_ref[e], e, expert)
    expert, position = expert[:tokens], position[:tokens]
    mix = 2.5 * scores / jnp.sum(scores, axis=1, keepdims=True)
    hits = jnp.zeros((tokens, rows), jnp.float32)
    weight = jnp.zeros((tokens, rows), jnp.float32)
    for k in range(routed):
        same = ids[:, k : k + 1] == expert
        hits = jnp.where(same, 1.0, hits)
        weight = jnp.where(same, mix[:, k : k + 1], weight)
    token = lax.broadcasted_iota(jnp.int32, (tokens, rows), 0)
    earlier = jnp.zeros((tokens, rows), jnp.float32)
    for t in range(tokens - 1):
        earlier = earlier + jnp.where(token > t, hits[t : t + 1], 0.0)
    place = jnp.where(earlier == position, hits, 0.0)
    return place, place * weight


def kernel(
    n, n_member, pieces, cap, experts,
    placement_ref, lengths_ref, ids_ref, scores_ref, x_ref,
    q_hbm, c_hbm, wg_hbm, wu_hbm, wd_hbm,
    latent_hbm, moe_ref,
    q_ref, c_ref, o_ref, wg_ref, wu_ref, wd_ref,
    xs_ref, send_ref, arr_ref, x2_ref, ag_ref, au_ref, inner_ref, yb_ref, ret_ref, mixw_ref, out_ref,
    q_sem, c_sem, o_sem, wg_sem, wu_sem, wd_sem,
    dsend_sem, drecv_sem, rsend_sem, rrecv_sem,
):
    side, member = lax.axis_index("side"), lax.axis_index("member")
    me = side * n_member + member
    tokens, width = x_ref.shape
    hidden = wg_hbm.shape[2]
    requests = q_hbm.shape[0]
    rows = pieces * n * cap
    per = n * cap
    nk = width // CHUNK

    def each_peer(visit):
        for step in range(n // n_member):
            there = lax.rem(side + step, n // n_member)

            @pl.loop(1 if step == 0 else 0, n_member)
            def _(i):
                other = lax.rem(member + i, n_member)
                visit(there * n_member + other, {"side": there, "member": other})

    def gate_copy(p, i):
        return pltpu.make_async_copy(
            wg_hbm.at[p, pl.ds(pl.multiple_of(i * CHUNK, CHUNK), CHUNK)], wg_ref.at[i], wg_sem.at[i]
        )

    def up_copy(p, i):
        return pltpu.make_async_copy(
            wu_hbm.at[p, pl.ds(pl.multiple_of(i * CHUNK, CHUNK), CHUNK)], wu_ref.at[i], wu_sem.at[i]
        )

    def down_copy(p, i):
        return pltpu.make_async_copy(
            wd_hbm.at[p, :, pl.ds(pl.multiple_of(i * CHUNK, CHUNK), CHUNK)], wd_ref.at[i], wd_sem.at[i]
        )

    barrier = pltpu.get_barrier_semaphore()

    each_peer(
        lambda d, where: pl.semaphore_signal(
            barrier, inc=1, device_id=where, device_id_type=MESH
        )
    )

    q_copy = pltpu.make_async_copy(q_hbm, q_ref, q_sem)
    c_copy = pltpu.make_async_copy(c_hbm, c_ref, c_sem)
    o_copy = pltpu.make_async_copy(o_ref, latent_hbm, o_sem)
    q_copy.start()
    c_copy.start()

    @pl.loop(0, nk)
    def _(i):
        gate_copy(0, i).start()
        up_copy(0, i).start()

    @pl.loop(0, nk)
    def _(i):
        down_copy(0, i).start()

    lanes = -(-rows // 128) * 128
    place, mixw = row_tables(
        placement_ref, ids_ref[...], scores_ref[...], n, pieces, cap, experts, lanes
    )
    high = mixw.astype(jnp.bfloat16)
    rest = mixw - high.astype(jnp.float32)
    mid = rest.astype(jnp.bfloat16)
    low = (rest - mid.astype(jnp.float32)).astype(jnp.bfloat16)
    pad = jnp.zeros((8 - tokens, lanes), jnp.float32)
    mixw_ref[...] = jnp.concatenate(
        [
            jnp.concatenate([v.astype(jnp.float32), pad], axis=0)
            for v in (high, mid, low, jnp.zeros_like(low))
        ],
        axis=0,
    ).astype(jnp.bfloat16)
    picks = jnp.concatenate([place, jnp.zeros((16 - tokens, lanes), jnp.float32)], axis=0)
    picks = picks.T.astype(jnp.bfloat16)
    xs_ref[...] = jnp.zeros_like(xs_ref)
    xs_ref[0:tokens, :] = x_ref[...]
    for p in range(pieces):
        for j in range(nk):
            cols = pl.ds(j * CHUNK, CHUNK)
            made = jnp.dot(
                picks[p * per : (p + 1) * per], xs_ref[:, cols], preferred_element_type=jnp.float32
            )
            send_ref[p, :, :, cols] = made.reshape(n, cap, CHUNK).astype(jnp.bfloat16)

    pl.semaphore_wait(barrier, n - 1)
    for p in range(pieces):

        def send_slots(d, where, p=p):
            pltpu.make_async_remote_copy(
                src_ref=send_ref.at[p, d],
                dst_ref=arr_ref.at[p, me],
                send_sem=dsend_sem.at[p],
                recv_sem=drecv_sem.at[p],
                device_id=where,
                device_id_type=MESH,
            ).start()

        each_peer(send_slots)
        arr_ref[p, me] = send_ref[p, me]

    q_copy.wait()
    c_copy.wait()
    scale = QK_DIM ** (-0.5)
    for r in range(requests):
        s = lax.dot_general(
            q_ref[r], c_ref[r], (((1,), (0,)), ((), ())), preferred_element_type=jnp.float32
        ) * scale
        valid = lax.broadcasted_iota(jnp.int32, s.shape, 1) < lengths_ref[r]
        s = jnp.where(valid, s, -jnp.inf)
        e = jnp.exp(s - jnp.max(s, axis=1, keepdims=True))
        a = (e / jnp.sum(e, axis=1, keepdims=True)).astype(jnp.bfloat16)
        o_ref[r] = lax.dot_general(
            a, c_ref[r, :LATENT], (((1,), (1,)), ((), ())), preferred_element_type=jnp.float32
        ).astype(jnp.bfloat16)
    o_copy.start()

    def drain(ref, sem):
        view = ref.at[pl.ds(0, n - 1)]
        pltpu.make_async_copy(view, view, sem).wait()

    cut = nk * 4 // 7
    groups = [[(0, nk)]] * (pieces - 1) + [[(0, cut), (cut, nk)]]

    def columns(group):
        return pl.ds(group[0] * CHUNK, (group[1] - group[0]) * CHUNK)

    def combine(p, j):
        got = ret_ref[p, :, :, pl.ds(j * CHUNK, CHUNK)]
        got = got.astype(jnp.float32).reshape(per, CHUNK).astype(jnp.bfloat16)
        part = jnp.dot(
            mixw_ref[:, p * per : (p + 1) * per], got, preferred_element_type=jnp.float32
        )
        return part[0:8] + part[8:16] + part[16:24]

    for p in range(pieces):
        drain(arr_ref.at[p], drecv_sem.at[p])
        for j in range(nk):
            cols = pl.ds(j * CHUNK, CHUNK)
            x2_ref[:, cols] = (
                arr_ref[p, :, :, cols].astype(jnp.float32).reshape(per, CHUNK).astype(jnp.bfloat16)
            )
        ag_ref[...] = jnp.zeros_like(ag_ref)
        au_ref[...] = jnp.zeros_like(au_ref)

        @pl.loop(0, nk)
        def _(i, p=p):
            xk = x2_ref[:, pl.ds(pl.multiple_of(i * CHUNK, CHUNK), CHUNK)]
            gate_copy(p, i).wait()
            ag_ref[...] += jnp.dot(xk, wg_ref[i], preferred_element_type=jnp.float32)
            if p + 1 < pieces:
                gate_copy(p + 1, i).start()
            up_copy(p, i).wait()
            au_ref[...] += jnp.dot(xk, wu_ref[i], preferred_element_type=jnp.float32)
            if p + 1 < pieces:
                up_copy(p + 1, i).start()

        g = ag_ref[...]
        inner_ref[...] = (g / (1.0 + jnp.exp(-g)) * au_ref[...]).astype(jnp.bfloat16)
        if p > 0:
            drain(ret_ref.at[p - 1], rrecv_sem.at[p - 1, 0])
            for j in range(nk):
                cols = pl.ds(j * CHUNK, CHUNK)
                before = 0.0 if p == 1 else out_ref[:, cols]
                out_ref[:, cols] = before + combine(p - 1, j)

        for g, group in enumerate(groups[p]):
            for j in range(*group):
                down_copy(p, j).wait()
                y = jnp.dot(inner_ref[...], wd_ref[j], preferred_element_type=jnp.float32)
                if p + 1 < pieces:
                    down_copy(p + 1, j).start()
                yb_ref[p, :, :, pl.ds(j * CHUNK, CHUNK)] = y.reshape(n, cap, CHUNK).astype(
                    jnp.bfloat16
                )
            cols = columns(group)

            def send_back(d, where, p=p, g=g, cols=cols):
                pltpu.make_async_remote_copy(
                    src_ref=yb_ref.at[p, d, :, cols],
                    dst_ref=ret_ref.at[p, me, :, cols],
                    send_sem=rsend_sem.at[p, g],
                    recv_sem=rrecv_sem.at[p, g],
                    device_id=where,
                    device_id_type=MESH,
                ).start()

            each_peer(send_back)
            ret_ref[p, me, :, cols] = yb_ref[p, me, :, cols]

    last = pieces - 1
    for g, group in enumerate(groups[last]):
        drain(ret_ref.at[last, :, :, columns(group)], rrecv_sem.at[last, g])
        for j in range(*group):
            cols = pl.ds(j * CHUNK, CHUNK)
            total = combine(last, j)
            if pieces > 1:
                total = total + out_ref[:, cols]
            moe_ref[:, cols] = total[0:tokens].astype(jnp.bfloat16)

    o_copy.wait()
    for p in range(pieces):
        drain(send_ref.at[p], dsend_sem.at[p])
        for g, group in enumerate(groups[p]):
            drain(yb_ref.at[p, :, :, columns(group)], rsend_sem.at[p, g])


def hand_over(latent_ref, moe_ref, latent_out_ref, moe_out_ref):
    latent_out_ref[...] = latent_ref[...]
    moe_out_ref[...] = moe_ref[...]


def shards(
    queries,
    latent_cache,
    lengths,
    moe_input,
    expert_ids,
    route_scores,
    placement,
    w_gate,
    w_up,
    w_down,
):
    n_side, n_member = lax.axis_size("side"), lax.axis_size("member")
    n = n_side * n_member
    pieces, width, hidden = w_gate.shape
    experts = placement.shape[0]
    tokens = moe_input.shape[0]
    cap = tokens * expert_ids.shape[1] // experts + 1
    per = n * cap
    rows = pieces * per
    lanes = -(-rows // 128) * 128
    nk = width // CHUNK
    requests, heads, entry = queries.shape
    cache_columns = jnp.swapaxes(latent_cache, 1, 2)
    bf16, f32 = jnp.bfloat16, jnp.float32
    vmem = pl.BlockSpec(memory_space=pltpu.VMEM)
    smem = pl.BlockSpec(memory_space=pltpu.SMEM)
    hbm = pl.BlockSpec(memory_space=pl.ANY)
    dma = pltpu.SemaphoreType.DMA
    latent_out, moe_out = pl.pallas_call(
        functools.partial(kernel, n, n_member, pieces, cap, experts),
        out_shape=(
            jax.ShapeDtypeStruct((requests, heads, LATENT), bf16),
            jax.ShapeDtypeStruct((tokens, width), bf16),
        ),
        in_specs=[smem, smem, vmem, vmem, vmem, hbm, hbm, hbm, hbm, hbm],
        out_specs=(hbm, vmem),
        scratch_shapes=[
            pltpu.VMEM(queries.shape, bf16),
            pltpu.VMEM(cache_columns.shape, bf16),
            pltpu.VMEM((requests, heads, LATENT), bf16),
            pltpu.VMEM((nk, CHUNK, hidden), bf16),
            pltpu.VMEM((nk, CHUNK, hidden), bf16),
            pltpu.VMEM((nk, hidden, CHUNK), bf16),
            pltpu.VMEM((16, width), bf16),
            pltpu.VMEM((pieces, n, cap, width), bf16),
            pltpu.VMEM((pieces, n, cap, width), bf16),
            pltpu.VMEM((per, width), bf16),
            pltpu.VMEM((per, hidden), f32),
            pltpu.VMEM((per, hidden), f32),
            pltpu.VMEM((per, hidden), bf16),
            pltpu.VMEM((pieces, n, cap, width), bf16),
            pltpu.VMEM((pieces, n, cap, width), bf16),
            pltpu.VMEM((32, lanes), bf16),
            pltpu.VMEM((8, width), f32),
            dma,
            dma,
            dma,
            dma((nk,)),
            dma((nk,)),
            dma((nk,)),
            dma((pieces,)),
            dma((pieces,)),
            dma((pieces, 2)),
            dma((pieces, 2)),
        ],
        compiler_params=pltpu.CompilerParams(
            collective_id=0, has_side_effects=True, vmem_limit_bytes=60 * 1024 * 1024
        ),
        cost_estimate=pl.CostEstimate(
            flops=6 * rows * width * hidden,
            bytes_accessed=6 * pieces * width * hidden,
            transcendentals=per * hidden,
        ),
    )(
        placement,
        lengths,
        expert_ids,
        route_scores,
        moe_input,
        queries,
        cache_columns,
        w_gate,
        w_up,
        w_down,
    )
    return pl.pallas_call(
        hand_over,
        out_shape=(
            jax.ShapeDtypeStruct(latent_out.shape, bf16),
            jax.ShapeDtypeStruct(moe_out.shape, bf16),
        ),
        in_specs=[vmem, vmem],
        out_specs=(vmem, vmem),
    )(latent_out, moe_out)


def solution(mesh):
    return jax.shard_map(
        shards,
        mesh=mesh,
        in_specs=(
            P(("groups", "side", "member"), None, None),
            P(("groups", "side", "member"), None, None),
            P(("groups", "side", "member")),
            P(("groups", "side", "member"), None),
            P(("groups", "side", "member"), None),
            P(("groups", "side", "member"), None),
            P(),
            P(("side", "member"), None, None),
            P(("side", "member"), None, None),
            P(("side", "member"), None, None),
        ),
        out_specs=(
            P(("groups", "side", "member"), None, None),
            P(("groups", "side", "member"), None),
        ),
        check_vma=False,
    )
```

```python
import functools

import jax
import jax.numpy as jnp
from jax import lax
from jax.experimental import pallas as pl
from jax.experimental.pallas import tpu as pltpu
from jax.sharding import PartitionSpec as P

LATENT = 512
QK_DIM = 192
CHUNK = 512
MESH = pl.DeviceIdType.MESH

def row_tables(placement_ref, ids, scores, n, pieces, cap, experts, rows):
    split = n * pieces // experts
    tokens, routed = ids.shape
    lanes = lax.broadcasted_iota(jnp.int32, (8, rows), 1).astype(jnp.float32)
    block = jnp.floor((lanes + 0.5) * (1.0 / cap))
    position = lanes - cap * block
    piece = jnp.floor((block + 0.5) * (1.0 / n))
    device = block - n * piece
    slot = jnp.floor((device * pieces + piece + 0.5) * (1.0 / split)).astype(jnp.int32)
    expert = jnp.full((8, rows), -1, jnp.int32)
    for e in range(experts):
        expert = jnp.where(slot == placement_ref[e], e, expert)
    expert, position = expert[:tokens], position[:tokens]
    mix = 2.5 * scores / jnp.sum(scores, axis=1, keepdims=True)
    hits = jnp.zeros((tokens, rows), jnp.float32)
    weight = jnp.zeros((tokens, rows), jnp.float32)
    for k in range(routed):
        same = ids[:, k : k + 1] == expert
        hits = jnp.where(same, 1.0, hits)
        weight = jnp.where(same, mix[:, k : k + 1], weight)
    token = lax.broadcasted_iota(jnp.int32, (tokens, rows), 0)
    earlier = jnp.zeros((tokens, rows), jnp.float32)
    for t in range(tokens - 1):
        earlier = earlier + jnp.where(token > t, hits[t : t + 1], 0.0)
    place = jnp.where(earlier == position, hits, 0.0)
    return place, place * weight

def kernel(
    n, n_member, pieces, cap, experts,
    placement_ref, lengths_ref, ids_ref, scores_ref, x_ref,
    q_hbm, c_hbm, wg_hbm, wu_hbm, wd_hbm,
    latent_hbm, moe_ref,
    q_ref, c_ref, o_ref, wg_ref, wu_ref, wd_ref,
    xs_ref, send_ref, arr_ref, x2_ref, ag_ref, au_ref, inner_ref, yb_ref, ret_ref, mixw_ref, out_ref,
    q_sem, c_sem, o_sem, wg_sem, wu_sem, wd_sem,
    dsend_sem, drecv_sem, rsend_sem, rrecv_sem,
):
    side, member = lax.axis_index("side"), lax.axis_index("member")
    me = side * n_member + member
    tokens, width = x_ref.shape
    hidden = wg_hbm.shape[2]
    requests = q_hbm.shape[0]
    rows = pieces * n * cap
    per = n * cap
    nk = width // CHUNK

    def each_peer(visit):
        for step in range(n // n_member):
            there = lax.rem(side + step, n // n_member)

            @pl.loop(1 if step == 0 else 0, n_member)
            def _(i):
                other = lax.rem(member + i, n_member)
                visit(there * n_member + other, {"side": there, "member": other})

    def gate_copy(p, i):
        return pltpu.make_async_copy(
            wg_hbm.at[p, pl.ds(pl.multiple_of(i * CHUNK, CHUNK), CHUNK)], wg_ref.at[i], wg_sem.at[i]
        )

    def up_copy(p, i):
        return pltpu.make_async_copy(
            wu_hbm.at[p, pl.ds(pl.multiple_of(i * CHUNK, CHUNK), CHUNK)], wu_ref.at[i], wu_sem.at[i]
        )

    def down_copy(p, i):
        return pltpu.make_async_copy(
            wd_hbm.at[p, :, pl.ds(pl.multiple_of(i * CHUNK, CHUNK), CHUNK)], wd_ref.at[i], wd_sem.at[i]
        )

    barrier = pltpu.get_barrier_semaphore()

    each_peer(
        lambda d, where: pl.semaphore_signal(
            barrier, inc=1, device_id=where, device_id_type=MESH
        )
    )

    q_copy = pltpu.make_async_copy(q_hbm, q_ref, q_sem)
    c_copy = pltpu.make_async_copy(c_hbm, c_ref, c_sem)
    o_copy = pltpu.make_async_copy(o_ref, latent_hbm, o_sem)
    q_copy.start()
    c_copy.start()

    @pl.loop(0, nk)
    def _(i):
        gate_copy(0, i).start()
        up_copy(0, i).start()

    @pl.loop(0, nk)
    def _(i):
        down_copy(0, i).start()

    lanes = -(-rows // 128) * 128
    place, mixw = row_tables(
        placement_ref, ids_ref[...], scores_ref[...], n, pieces, cap, experts, lanes
    )
    high = mixw.astype(jnp.bfloat16)
    rest = mixw - high.astype(jnp.float32)
    mid = rest.astype(jnp.bfloat16)
    low = (rest - mid.astype(jnp.float32)).astype(jnp.bfloat16)
    pad = jnp.zeros((8 - tokens, lanes), jnp.float32)
    mixw_ref[...] = jnp.concatenate(
        [
            jnp.concatenate([v.astype(jnp.float32), pad], axis=0)
            for v in (high, mid, low, jnp.zeros_like(low))
        ],
        axis=0,
    ).astype(jnp.bfloat16)
    picks = jnp.concatenate([place, jnp.zeros((16 - tokens, lanes), jnp.float32)], axis=0)
    picks = picks.T.astype(jnp.bfloat16)
    xs_ref[...] = jnp.zeros_like(xs_ref)
    xs_ref[0:tokens, :] = x_ref[...]
    for p in range(pieces):
        for j in range(nk):
            cols = pl.ds(j * CHUNK, CHUNK)
            made = jnp.dot(
                picks[p * per : (p + 1) * per], xs_ref[:, cols], preferred_element_type=jnp.float32
            )
            send_ref[p, :, :, cols] = made.reshape(n, cap, CHUNK).astype(jnp.bfloat16)

    cut, far = nk * 2 // 7, nk * 4 // 7

    out_groups = [[(0, cut), (cut, far), (far, nk)]] + [[(0, nk)]] * (pieces - 1)
    groups = [[(0, nk)]] * (pieces - 1) + [[(0, far), (far, nk)]]

    def columns(group):
        return pl.ds(group[0] * CHUNK, (group[1] - group[0]) * CHUNK)

    pl.semaphore_wait(barrier, n - 1)
    for p in range(pieces):
        for g, group in enumerate(out_groups[p]):
            cols = columns(group)

            def send_slots(d, where, p=p, g=g, cols=cols):
                pltpu.make_async_remote_copy(
                    src_ref=send_ref.at[p, d, :, cols],
                    dst_ref=arr_ref.at[p, me, :, cols],
                    send_sem=dsend_sem.at[p, g],
                    recv_sem=drecv_sem.at[p, g],
                    device_id=where,
                    device_id_type=MESH,
                ).start()

            each_peer(send_slots)
        arr_ref[p, me] = send_ref[p, me]

    q_copy.wait()
    c_copy.wait()
    scale = QK_DIM ** (-0.5)
    for r in range(requests):
        s = lax.dot_general(
            q_ref[r], c_ref[r], (((1,), (0,)), ((), ())), preferred_element_type=jnp.float32
        ) * scale
        valid = lax.broadcasted_iota(jnp.int32, s.shape, 1) < lengths_ref[r]
        s = jnp.where(valid, s, -jnp.inf)
        e = jnp.exp(s - jnp.max(s, axis=1, keepdims=True))
        a = (e / jnp.sum(e, axis=1, keepdims=True)).astype(jnp.bfloat16)
        o_ref[r] = lax.dot_general(
            a, c_ref[r, :LATENT], (((1,), (1,)), ((), ())), preferred_element_type=jnp.float32
        ).astype(jnp.bfloat16)
    o_copy.start()

    def drain(ref, sem):
        view = ref.at[pl.ds(0, n - 1)]
        pltpu.make_async_copy(view, view, sem).wait()

    def combine(p, j):
        got = ret_ref[p, :, :, pl.ds(j * CHUNK, CHUNK)]
        got = got.astype(jnp.float32).reshape(per, CHUNK).astype(jnp.bfloat16)
        part = jnp.dot(
            mixw_ref[:, p * per : (p + 1) * per], got, preferred_element_type=jnp.float32
        )
        return part[0:8] + part[8:16] + part[16:24]

    for p in range(pieces):
        ag_ref[...] = jnp.zeros_like(ag_ref)
        au_ref[...] = jnp.zeros_like(au_ref)
        for g, group in enumerate(out_groups[p]):
            drain(arr_ref.at[p, :, :, columns(group)], drecv_sem.at[p, g])
            for j in range(*group):
                cols = pl.ds(j * CHUNK, CHUNK)
                x2_ref[:, cols] = (
                    arr_ref[p, :, :, cols].astype(jnp.float32).reshape(per, CHUNK).astype(jnp.bfloat16)
                )

            @pl.loop(*group)
            def _(i, p=p):
                xk = x2_ref[:, pl.ds(pl.multiple_of(i * CHUNK, CHUNK), CHUNK)]
                gate_copy(p, i).wait()
                ag_ref[...] += jnp.dot(xk, wg_ref[i], preferred_element_type=jnp.float32)
                if p + 1 < pieces:
                    gate_copy(p + 1, i).start()
                up_copy(p, i).wait()
                au_ref[...] += jnp.dot(xk, wu_ref[i], preferred_element_type=jnp.float32)
                if p + 1 < pieces:
                    up_copy(p + 1, i).start()

        g = ag_ref[...]
        inner_ref[...] = (g / (1.0 + jnp.exp(-g)) * au_ref[...]).astype(jnp.bfloat16)
        if p > 0:
            drain(ret_ref.at[p - 1], rrecv_sem.at[p - 1, 0])
            for j in range(nk):
                cols = pl.ds(j * CHUNK, CHUNK)
                before = 0.0 if p == 1 else out_ref[:, cols]
                out_ref[:, cols] = before + combine(p - 1, j)

        for g, group in enumerate(groups[p]):
            for j in range(*group):
                down_copy(p, j).wait()
                y = jnp.dot(inner_ref[...], wd_ref[j], preferred_element_type=jnp.float32)
                if p + 1 < pieces:
                    down_copy(p + 1, j).start()
                yb_ref[p, :, :, pl.ds(j * CHUNK, CHUNK)] = y.reshape(n, cap, CHUNK).astype(
                    jnp.bfloat16
                )
            cols = columns(group)

            def send_back(d, where, p=p, g=g, cols=cols):
                pltpu.make_async_remote_copy(
                    src_ref=yb_ref.at[p, d, :, cols],
                    dst_ref=ret_ref.at[p, me, :, cols],
                    send_sem=rsend_sem.at[p, g],
                    recv_sem=rrecv_sem.at[p, g],
                    device_id=where,
                    device_id_type=MESH,
                ).start()

            each_peer(send_back)
            ret_ref[p, me, :, cols] = yb_ref[p, me, :, cols]

    last = pieces - 1
    for g, group in enumerate(groups[last]):
        drain(ret_ref.at[last, :, :, columns(group)], rrecv_sem.at[last, g])
        for j in range(*group):
            cols = pl.ds(j * CHUNK, CHUNK)
            total = combine(last, j)
            if pieces > 1:
                total = total + out_ref[:, cols]
            moe_ref[:, cols] = total[0:tokens].astype(jnp.bfloat16)

    o_copy.wait()
    for p in range(pieces):
        for g, group in enumerate(out_groups[p]):
            drain(send_ref.at[p, :, :, columns(group)], dsend_sem.at[p, g])
        for g, group in enumerate(groups[p]):
            drain(yb_ref.at[p, :, :, columns(group)], rsend_sem.at[p, g])

def hand_over(latent_ref, moe_ref, latent_out_ref, moe_out_ref):
    latent_out_ref[...] = latent_ref[...]
    moe_out_ref[...] = moe_ref[...]

def shards(
    queries,
    latent_cache,
    lengths,
    moe_input,
    expert_ids,
    route_scores,
    placement,
    w_gate,
    w_up,
    w_down,
):
    n_side, n_member = lax.axis_size("side"), lax.axis_size("member")
    n = n_side * n_member
    pieces, width, hidden = w_gate.shape
    experts = placement.shape[0]
    tokens = moe_input.shape[0]
    cap = tokens * expert_ids.shape[1] // experts + 1
    per = n * cap
    rows = pieces * per
    lanes = -(-rows // 128) * 128
    nk = width // CHUNK
    requests, heads, entry = queries.shape
    cache_columns = jnp.swapaxes(latent_cache, 1, 2)
    bf16, f32 = jnp.bfloat16, jnp.float32
    vmem = pl.BlockSpec(memory_space=pltpu.VMEM)
    smem = pl.BlockSpec(memory_space=pltpu.SMEM)
    hbm = pl.BlockSpec(memory_space=pl.ANY)
    dma = pltpu.SemaphoreType.DMA
    latent_out, moe_out = pl.pallas_call(
        functools.partial(kernel, n, n_member, pieces, cap, experts),
        out_shape=(
            jax.ShapeDtypeStruct((requests, heads, LATENT), bf16),
            jax.ShapeDtypeStruct((tokens, width), bf16),
        ),
        in_specs=[smem, smem, vmem, vmem, vmem, hbm, hbm, hbm, hbm, hbm],
        out_specs=(hbm, vmem),
        scratch_shapes=[
            pltpu.VMEM(queries.shape, bf16),
            pltpu.VMEM(cache_columns.shape, bf16),
            pltpu.VMEM((requests, heads, LATENT), bf16),
            pltpu.VMEM((nk, CHUNK, hidden), bf16),
            pltpu.VMEM((nk, CHUNK, hidden), bf16),
            pltpu.VMEM((nk, hidden, CHUNK), bf16),
            pltpu.VMEM((16, width), bf16),
            pltpu.VMEM((pieces, n, cap, width), bf16),
            pltpu.VMEM((pieces, n, cap, width), bf16),
            pltpu.VMEM((per, width), bf16),
            pltpu.VMEM((per, hidden), f32),
            pltpu.VMEM((per, hidden), f32),
            pltpu.VMEM((per, hidden), bf16),
            pltpu.VMEM((pieces, n, cap, width), bf16),
            pltpu.VMEM((pieces, n, cap, width), bf16),
            pltpu.VMEM((32, lanes), bf16),
            pltpu.VMEM((8, width), f32),
            dma,
            dma,
            dma,
            dma((nk,)),
            dma((nk,)),
            dma((nk,)),
            dma((pieces, 3)),
            dma((pieces, 3)),
            dma((pieces, 3)),
            dma((pieces, 3)),
        ],
        compiler_params=pltpu.CompilerParams(
            collective_id=0, has_side_effects=True, vmem_limit_bytes=60 * 1024 * 1024
        ),
        cost_estimate=pl.CostEstimate(
            flops=6 * rows * width * hidden,
            bytes_accessed=6 * pieces * width * hidden,
            transcendentals=per * hidden,
        ),
    )(
        placement,
        lengths,
        expert_ids,
        route_scores,
        moe_input,
        queries,
        cache_columns,
        w_gate,
        w_up,
        w_down,
    )
    return pl.pallas_call(
        hand_over,
        out_shape=(
            jax.ShapeDtypeStruct(latent_out.shape, bf16),
            jax.ShapeDtypeStruct(moe_out.shape, bf16),
        ),
        in_specs=[vmem, vmem],
        out_specs=(vmem, vmem),
    )(latent_out, moe_out)

def solution(mesh):
    return jax.shard_map(
        shards,
        mesh=mesh,
        in_specs=(
            P(("groups", "side", "member"), None, None),
            P(("groups", "side", "member"), None, None),
            P(("groups", "side", "member")),
            P(("groups", "side", "member"), None),
            P(("groups", "side", "member"), None),
            P(("groups", "side", "member"), None),
            P(),
            P(("side", "member"), None, None),
            P(("side", "member"), None, None),
            P(("side", "member"), None, None),
        ),
        out_specs=(
            P(("groups", "side", "member"), None, None),
            P(("groups", "side", "member"), None),
        ),
        check_vma=False,
    )
```

```python
import functools

import jax
import jax.numpy as jnp
from jax import lax
from jax.experimental import pallas as pl
from jax.experimental.pallas import tpu as pltpu
from jax.sharding import PartitionSpec as P

LATENT = 512
QK_DIM = 192
CHUNK = 512
MESH = pl.DeviceIdType.MESH

def row_tables(placement_ref, ids, scores, n, pieces, cap, experts, rows):
    split = n * pieces // experts
    tokens, routed = ids.shape
    lanes = lax.broadcasted_iota(jnp.int32, (8, rows), 1).astype(jnp.float32)
    block = jnp.floor((lanes + 0.5) * (1.0 / cap))
    position = lanes - cap * block
    piece = jnp.floor((block + 0.5) * (1.0 / n))
    device = block - n * piece
    slot = jnp.floor((device * pieces + piece + 0.5) * (1.0 / split)).astype(jnp.int32)
    expert = jnp.full((8, rows), -1, jnp.int32)
    for e in range(experts):
        expert = jnp.where(slot == placement_ref[e], e, expert)
    expert, position = expert[:tokens], position[:tokens]
    mix = 2.5 * scores / jnp.sum(scores, axis=1, keepdims=True)
    hits = jnp.zeros((tokens, rows), jnp.float32)
    weight = jnp.zeros((tokens, rows), jnp.float32)
    for k in range(routed):
        same = ids[:, k : k + 1] == expert
        hits = jnp.where(same, 1.0, hits)
        weight = jnp.where(same, mix[:, k : k + 1], weight)
    token = lax.broadcasted_iota(jnp.int32, (tokens, rows), 0)
    earlier = jnp.zeros((tokens, rows), jnp.float32)
    for t in range(tokens - 1):
        earlier = earlier + jnp.where(token > t, hits[t : t + 1], 0.0)
    place = jnp.where(earlier == position, hits, 0.0)
    return place, place * weight

def kernel(
    n, n_member, pieces, cap, experts,
    placement_ref, lengths_ref, ids_ref, scores_ref, x_ref,
    q_hbm, c_hbm, wg_hbm, wu_hbm, wd_hbm,
    latent_hbm, moe_ref,
    q_ref, c_ref, o_ref, wg_ref, wu_ref, wd_ref,
    xs_ref, send_ref, arr_ref, x2_ref, ag_ref, au_ref, inner_ref, yb_ref, ret_ref, mixw_ref, out_ref,
    q_sem, c_sem, o_sem, wg_sem, wu_sem, wd_sem,
    dsend_sem, drecv_sem, rsend_sem, rrecv_sem,
):
    side, member = lax.axis_index("side"), lax.axis_index("member")
    me = side * n_member + member
    tokens, width = x_ref.shape
    hidden = wg_hbm.shape[2]
    requests = q_hbm.shape[0]
    rows = pieces * n * cap
    per = n * cap
    nk = width // CHUNK

    def each_peer(visit):
        for step in range(n // n_member):
            there = lax.rem(side + step, n // n_member)

            @pl.loop(1 if step == 0 else 0, n_member)
            def _(i):
                other = lax.rem(member + i, n_member)
                visit(there * n_member + other, {"side": there, "member": other})

    def gate_copy(p, i):
        return pltpu.make_async_copy(
            wg_hbm.at[p, pl.ds(pl.multiple_of(i * CHUNK, CHUNK), CHUNK)], wg_ref.at[i], wg_sem.at[i]
        )

    def up_copy(p, i):
        return pltpu.make_async_copy(
            wu_hbm.at[p, pl.ds(pl.multiple_of(i * CHUNK, CHUNK), CHUNK)], wu_ref.at[i], wu_sem.at[i]
        )

    def down_copy(p, i):
        return pltpu.make_async_copy(
            wd_hbm.at[p, :, pl.ds(pl.multiple_of(i * CHUNK, CHUNK), CHUNK)], wd_ref.at[i], wd_sem.at[i]
        )

    barrier = pltpu.get_barrier_semaphore()

    each_peer(
        lambda d, where: pl.semaphore_signal(
            barrier, inc=1, device_id=where, device_id_type=MESH
        )
    )

    q_copy = pltpu.make_async_copy(q_hbm, q_ref, q_sem)
    c_copy = pltpu.make_async_copy(c_hbm, c_ref, c_sem)
    o_copy = pltpu.make_async_copy(o_ref, latent_hbm, o_sem)
    q_copy.start()
    c_copy.start()

    @pl.loop(0, nk)
    def _(i):
        gate_copy(0, i).start()
        up_copy(0, i).start()

    @pl.loop(0, nk)
    def _(i):
        down_copy(0, i).start()

    lanes = -(-rows // 128) * 128
    place, mixw = row_tables(
        placement_ref, ids_ref[...], scores_ref[...], n, pieces, cap, experts, lanes
    )
    high = mixw.astype(jnp.bfloat16)
    rest = mixw - high.astype(jnp.float32)
    mid = rest.astype(jnp.bfloat16)
    low = (rest - mid.astype(jnp.float32)).astype(jnp.bfloat16)
    pad = jnp.zeros((8 - tokens, lanes), jnp.float32)
    mixw_ref[...] = jnp.concatenate(
        [
            jnp.concatenate([v.astype(jnp.float32), pad], axis=0)
            for v in (high, mid, low, jnp.zeros_like(low))
        ],
        axis=0,
    ).astype(jnp.bfloat16)
    picks = jnp.concatenate([place, jnp.zeros((16 - tokens, lanes), jnp.float32)], axis=0)
    picks = picks.T.astype(jnp.bfloat16)
    xs_ref[...] = jnp.zeros_like(xs_ref)
    xs_ref[0:tokens, :] = x_ref[...]
    for p in range(pieces):
        for j in range(nk):
            cols = pl.ds(j * CHUNK, CHUNK)
            made = jnp.dot(
                picks[p * per : (p + 1) * per], xs_ref[:, cols], preferred_element_type=jnp.float32
            )
            send_ref[p, :, :, cols] = made.reshape(n, cap, CHUNK).astype(jnp.bfloat16)

    first, cut, far = nk // 7, nk * 2 // 7, nk * 4 // 7

    out_groups = [[(0, first), (first, cut), (cut, far), (far, nk)]] + [[(0, nk)]] * (pieces - 1)
    groups = [[(0, nk)]] * (pieces - 1) + [[(0, far), (far, nk)]]

    def columns(group):
        return pl.ds(group[0] * CHUNK, (group[1] - group[0]) * CHUNK)

    pl.semaphore_wait(barrier, n - 1)
    for p in range(pieces):
        for g, group in enumerate(out_groups[p]):
            cols = columns(group)

            def send_slots(d, where, p=p, g=g, cols=cols):
                pltpu.make_async_remote_copy(
                    src_ref=send_ref.at[p, d, :, cols],
                    dst_ref=arr_ref.at[p, me, :, cols],
                    send_sem=dsend_sem.at[p, g],
                    recv_sem=drecv_sem.at[p, g],
                    device_id=where,
                    device_id_type=MESH,
                ).start()

            each_peer(send_slots)
        arr_ref[p, me] = send_ref[p, me]

    q_copy.wait()
    c_copy.wait()
    scale = QK_DIM ** (-0.5)
    for r in range(requests):
        s = lax.dot_general(
            q_ref[r], c_ref[r], (((1,), (0,)), ((), ())), preferred_element_type=jnp.float32
        ) * scale
        valid = lax.broadcasted_iota(jnp.int32, s.shape, 1) < lengths_ref[r]
        s = jnp.where(valid, s, -jnp.inf)
        e = jnp.exp(s - jnp.max(s, axis=1, keepdims=True))
        a = (e / jnp.sum(e, axis=1, keepdims=True)).astype(jnp.bfloat16)
        o_ref[r] = lax.dot_general(
            a, c_ref[r, :LATENT], (((1,), (1,)), ((), ())), preferred_element_type=jnp.float32
        ).astype(jnp.bfloat16)
    o_copy.start()

    def drain(ref, sem):
        view = ref.at[pl.ds(0, n - 1)]
        pltpu.make_async_copy(view, view, sem).wait()

    def combine(p, j):
        got = ret_ref[p, :, :, pl.ds(j * CHUNK, CHUNK)]
        got = got.astype(jnp.float32).reshape(per, CHUNK).astype(jnp.bfloat16)
        part = jnp.dot(
            mixw_ref[:, p * per : (p + 1) * per], got, preferred_element_type=jnp.float32
        )
        return part[0:8] + part[8:16] + part[16:24]

    for p in range(pieces):
        ag_ref[...] = jnp.zeros_like(ag_ref)
        au_ref[...] = jnp.zeros_like(au_ref)
        for g, group in enumerate(out_groups[p]):
            drain(arr_ref.at[p, :, :, columns(group)], drecv_sem.at[p, g])
            for j in range(*group):
                cols = pl.ds(j * CHUNK, CHUNK)
                x2_ref[:, cols] = (
                    arr_ref[p, :, :, cols].astype(jnp.float32).reshape(per, CHUNK).astype(jnp.bfloat16)
                )

            @pl.loop(*group)
            def _(i, p=p):
                xk = x2_ref[:, pl.ds(pl.multiple_of(i * CHUNK, CHUNK), CHUNK)]
                gate_copy(p, i).wait()
                ag_ref[...] += jnp.dot(xk, wg_ref[i], preferred_element_type=jnp.float32)
                if p + 1 < pieces:
                    gate_copy(p + 1, i).start()
                up_copy(p, i).wait()
                au_ref[...] += jnp.dot(xk, wu_ref[i], preferred_element_type=jnp.float32)
                if p + 1 < pieces:
                    up_copy(p + 1, i).start()

        g = ag_ref[...]
        inner_ref[...] = (g / (1.0 + jnp.exp(-g)) * au_ref[...]).astype(jnp.bfloat16)
        if p > 0:
            drain(ret_ref.at[p - 1], rrecv_sem.at[p - 1, 0])
            for j in range(nk):
                cols = pl.ds(j * CHUNK, CHUNK)
                before = 0.0 if p == 1 else out_ref[:, cols]
                out_ref[:, cols] = before + combine(p - 1, j)

        for g, group in enumerate(groups[p]):
            for j in range(*group):
                down_copy(p, j).wait()
                y = jnp.dot(inner_ref[...], wd_ref[j], preferred_element_type=jnp.float32)
                if p + 1 < pieces:
                    down_copy(p + 1, j).start()
                yb_ref[p, :, :, pl.ds(j * CHUNK, CHUNK)] = y.reshape(n, cap, CHUNK).astype(
                    jnp.bfloat16
                )
            cols = columns(group)

            def send_back(d, where, p=p, g=g, cols=cols):
                pltpu.make_async_remote_copy(
                    src_ref=yb_ref.at[p, d, :, cols],
                    dst_ref=ret_ref.at[p, me, :, cols],
                    send_sem=rsend_sem.at[p, g],
                    recv_sem=rrecv_sem.at[p, g],
                    device_id=where,
                    device_id_type=MESH,
                ).start()

            each_peer(send_back)
            ret_ref[p, me, :, cols] = yb_ref[p, me, :, cols]

    last = pieces - 1
    for g, group in enumerate(groups[last]):
        drain(ret_ref.at[last, :, :, columns(group)], rrecv_sem.at[last, g])
        for j in range(*group):
            cols = pl.ds(j * CHUNK, CHUNK)
            total = combine(last, j)
            if pieces > 1:
                total = total + out_ref[:, cols]
            moe_ref[:, cols] = total[0:tokens].astype(jnp.bfloat16)

    o_copy.wait()
    for p in range(pieces):
        for g, group in enumerate(out_groups[p]):
            drain(send_ref.at[p, :, :, columns(group)], dsend_sem.at[p, g])
        for g, group in enumerate(groups[p]):
            drain(yb_ref.at[p, :, :, columns(group)], rsend_sem.at[p, g])

def hand_over(latent_ref, moe_ref, latent_out_ref, moe_out_ref):
    latent_out_ref[...] = latent_ref[...]
    moe_out_ref[...] = moe_ref[...]

def shards(
    queries,
    latent_cache,
    lengths,
    moe_input,
    expert_ids,
    route_scores,
    placement,
    w_gate,
    w_up,
    w_down,
):
    n_side, n_member = lax.axis_size("side"), lax.axis_size("member")
    n = n_side * n_member
    pieces, width, hidden = w_gate.shape
    experts = placement.shape[0]
    tokens = moe_input.shape[0]
    cap = tokens * expert_ids.shape[1] // experts + 1
    per = n * cap
    rows = pieces * per
    lanes = -(-rows // 128) * 128
    nk = width // CHUNK
    requests, heads, entry = queries.shape
    cache_columns = jnp.swapaxes(latent_cache, 1, 2)
    bf16, f32 = jnp.bfloat16, jnp.float32
    vmem = pl.BlockSpec(memory_space=pltpu.VMEM)
    smem = pl.BlockSpec(memory_space=pltpu.SMEM)
    hbm = pl.BlockSpec(memory_space=pl.ANY)
    dma = pltpu.SemaphoreType.DMA
    latent_out, moe_out = pl.pallas_call(
        functools.partial(kernel, n, n_member, pieces, cap, experts),
        out_shape=(
            jax.ShapeDtypeStruct((requests, heads, LATENT), bf16),
            jax.ShapeDtypeStruct((tokens, width), bf16),
        ),
        in_specs=[smem, smem, vmem, vmem, vmem, hbm, hbm, hbm, hbm, hbm],
        out_specs=(hbm, vmem),
        scratch_shapes=[
            pltpu.VMEM(queries.shape, bf16),
            pltpu.VMEM(cache_columns.shape, bf16),
            pltpu.VMEM((requests, heads, LATENT), bf16),
            pltpu.VMEM((nk, CHUNK, hidden), bf16),
            pltpu.VMEM((nk, CHUNK, hidden), bf16),
            pltpu.VMEM((nk, hidden, CHUNK), bf16),
            pltpu.VMEM((16, width), bf16),
            pltpu.VMEM((pieces, n, cap, width), bf16),
            pltpu.VMEM((pieces, n, cap, width), bf16),
            pltpu.VMEM((per, width), bf16),
            pltpu.VMEM((per, hidden), f32),
            pltpu.VMEM((per, hidden), f32),
            pltpu.VMEM((per, hidden), bf16),
            pltpu.VMEM((pieces, n, cap, width), bf16),
            pltpu.VMEM((pieces, n, cap, width), bf16),
            pltpu.VMEM((32, lanes), bf16),
            pltpu.VMEM((8, width), f32),
            dma,
            dma,
            dma,
            dma((nk,)),
            dma((nk,)),
            dma((nk,)),
            dma((pieces, 4)),
            dma((pieces, 4)),
            dma((pieces, 4)),
            dma((pieces, 4)),
        ],
        compiler_params=pltpu.CompilerParams(
            collective_id=0, has_side_effects=True, vmem_limit_bytes=60 * 1024 * 1024
        ),
        cost_estimate=pl.CostEstimate(
            flops=6 * rows * width * hidden,
            bytes_accessed=6 * pieces * width * hidden,
            transcendentals=per * hidden,
        ),
    )(
        placement,
        lengths,
        expert_ids,
        route_scores,
        moe_input,
        queries,
        cache_columns,
        w_gate,
        w_up,
        w_down,
    )
    return pl.pallas_call(
        hand_over,
        out_shape=(
            jax.ShapeDtypeStruct(latent_out.shape, bf16),
            jax.ShapeDtypeStruct(moe_out.shape, bf16),
        ),
        in_specs=[vmem, vmem],
        out_specs=(vmem, vmem),
    )(latent_out, moe_out)

def solution(mesh):
    return jax.shard_map(
        shards,
        mesh=mesh,
        in_specs=(
            P(("groups", "side", "member"), None, None),
            P(("groups", "side", "member"), None, None),
            P(("groups", "side", "member")),
            P(("groups", "side", "member"), None),
            P(("groups", "side", "member"), None),
            P(("groups", "side", "member"), None),
            P(),
            P(("side", "member"), None, None),
            P(("side", "member"), None, None),
            P(("side", "member"), None, None),
        ),
        out_specs=(
            P(("groups", "side", "member"), None, None),
            P(("groups", "side", "member"), None),
        ),
        check_vma=False,
    )
```
